32 devices in a mesh: fsdp: 4 (over z), ctx: 2 (over x), tp: 4 (over y, core).
Axes of the slice: x: 2, y: 2, z: 4, core: 2. Of those that a mesh axis runs over, the one named last changes fastest.
Arguments:
- tokens: bfloat16 [4, 1024, 1024], P('fsdp', 'ctx'), may hold values from -6 to 6
- lengths: int32 [4], P('fsdp'), may hold values from 512 to 1024, as said below
- cotangent: bfloat16 [4, 1024, 1024], P('fsdp', 'ctx'), may hold values from -6 to 6
- in_norm_gain: bfloat16 [1024], P(('fsdp', 'ctx')), may hold values from 0.5 to 1.5
- ffn_norm_gain: bfloat16 [1024], P(('fsdp', 'ctx')), may hold values from 0.099609375 to 1.8984375
- mixer_in: bfloat16 [1024, 2, 1536], P(('fsdp', 'ctx'), None, 'tp'), may hold values from -0.1875 to 0.1875
- step_weight: bfloat16 [1024, 24], P(('fsdp', 'ctx'), 'tp'), may hold values from -0.1875 to 0.1875
- state_proj: bfloat16 [1024, 256], P(('fsdp', 'ctx')), may hold values from -0.0078125 to 0.0078125
- keyval_weight: bfloat16 [1024, 256], P(('fsdp', 'ctx')), may hold values from -0.1875 to 0.1875
- query_weight: bfloat16 [1024, 512], P(('fsdp', 'ctx'), 'tp'), may hold values from -0.1875 to 0.1875
- step_bias: float32 [24], P('tp'), may hold values from -2 to 1
- decay_log: float32 [24], P('tp'), may hold values from -12 to -2.5
- skip_gain: float32 [24], P('tp'), may hold values from 0.5 to 1.5
- mixer_out: bfloat16 [1536, 1024], P('tp', ('fsdp', 'ctx')), may hold values from -0.15625 to 0.15625
- attn_out: bfloat16 [512, 1024], P('tp', ('fsdp', 'ctx')), may hold values from -0.75 to 0.75
- ffn_gate: bfloat16 [1024, 2048], P(('fsdp', 'ctx'), 'tp'), may hold values from -0.1875 to 0.1875
- ffn_up: bfloat16 [1024, 2048], P(('fsdp', 'ctx'), 'tp'), may hold values from -0.1875 to 0.1875
- ffn_down: bfloat16 [2048, 1024], P('tp', ('fsdp', 'ctx')), may hold values from -0.25 to 0.25
Outputs:
- block_out: bfloat16 [4, 1024, 1024], P('fsdp', 'ctx')
- input_grad: float32 [4, 1024, 1024], P('fsdp', 'ctx')
- in_norm_grad: float32 [1024], P(('fsdp', 'ctx'))
- ffn_norm_grad: float32 [1024], P(('fsdp', 'ctx'))
- mixer_in_grad: float32 [1024, 2, 1536], P(('fsdp', 'ctx'), None, 'tp')
- step_weight_grad: float32 [1024, 24], P(('fsdp', 'ctx'), 'tp')
- state_proj_grad: float32 [1024, 256], P(('fsdp', 'ctx'))
- keyval_grad: float32 [1024, 256], P(('fsdp', 'ctx'))
- query_grad: float32 [1024, 512], P(('fsdp', 'ctx'), 'tp')
- step_bias_grad: float32 [24], P('tp')
- decay_log_grad: float32 [24], P('tp')
- skip_gain_grad: float32 [24], P('tp')
- mixer_out_grad: float32 [1536, 1024], P('tp', ('fsdp', 'ctx'))
- attn_out_grad: float32 [512, 1024], P('tp', ('fsdp', 'ctx'))
- gate_grad: float32 [1024, 2048], P(('fsdp', 'ctx'), 'tp')
- up_grad: float32 [1024, 2048], P(('fsdp', 'ctx'), 'tp')
- down_grad: float32 [2048, 1024], P('tp', ('fsdp', 'ctx'))
The draws below stay inside these ranges and needn't reach their ends.
Inputs may be any that keep to these rules, and one draw needn't show every extreme that they name: `lengths`: each sequence's live positions; in every draw one sequence has all 1024 live.
All inputs are finite; a program needn't handle non-finite values.
Results may differ from the reference program's by a relative error of at most 0.035.
Values may be sent and summed in bfloat16 or wider, within the bound.
A program may use at most 128 MiB of HBM per device.

```python
import jax
import jax.numpy as jnp
from jax import lax

D = 1024
FF = 2048
MHEADS = 24
MDIM = 64
STATE = 128
QHEADS = 8
KVHEADS = 2
HDIM = 64
STRETCH = 256
SEQ_LEN = 1024
BATCH = 4
MINNER = 1536
N_TP = 4


def draw_lengths(key, part):
    drawn = jax.random.randint(key, (BATCH,), SEQ_LEN // 2, SEQ_LEN + 1, dtype=jnp.int32)
    chosen = jax.random.randint(jax.random.fold_in(key, 11), (), 0, BATCH, dtype=jnp.int32)
    return jnp.where(jnp.arange(BATCH, dtype=jnp.int32) == chosen, SEQ_LEN, drawn).astype(jnp.int32)


def level_of(stream_key, dims, cuts, least, high):
    gain = 1.0
    for dim, blocks in cuts:
        draws = jax.random.uniform(jax.random.fold_in(jax.random.fold_in(stream_key, 6), dim), (blocks,), jnp.float32, least / len(cuts), high / len(cuts))
        gain = gain * jnp.repeat(jnp.exp(draws), dims[dim] // blocks).reshape((-1,) + (1,) * (len(dims) - 1 - dim))
    return gain


def normal_values(rng, extent, scale, bound, split=(), kind=jnp.bfloat16):
    factor_of = level_of(rng, extent, split, -0.22, 0.18) if split else 1.0
    entries = jax.random.normal(rng, extent, jnp.float32) * scale * factor_of
    return jnp.minimum(jnp.maximum(entries, -bound), bound).astype(kind)


def setup_inputs(seed: int = 0) -> dict:
    splits = jax.random.split(jax.random.key(seed), 19)
    tokens = normal_values(splits[0], (BATCH, SEQ_LEN, D), 1.0, 6.0, ((0, 4), (1, 2)))
    lengths = draw_lengths(jax.random.fold_in(splits[18], 71), 0)
    cotangent = normal_values(splits[2], (BATCH, SEQ_LEN, D), 1.0, 6.0, ((0, 4), (1, 2)))
    in_norm_gain = jnp.clip(1.0 + 0.1 * jax.random.normal(splits[3], (D,), jnp.float32), 0.5, 1.5).astype(jnp.bfloat16)
    ffn_norm_gain = jnp.clip(1.0 + 0.18 * jax.random.normal(splits[4], (D,), jnp.float32), 0.099609375, 1.8984375).astype(jnp.bfloat16)
    mixer_in = normal_values(splits[5], (D, 2, MINNER), D ** -0.5, 0.1875, ((0, 8), (2, 4)))
    step_weight = normal_values(splits[6], (D, MHEADS), D ** -0.5, 0.1875, ((0, 8), (1, 4)))
    state_proj = normal_values(splits[7], (D, 2 * STATE), (D * 512) ** -0.5, 0.0078125, ((0, 8),))
    keyval_weight = normal_values(splits[8], (D, 2 * KVHEADS * HDIM), D ** -0.5, 0.1875, ((0, 8),))
    query_weight = normal_values(splits[9], (D, QHEADS * HDIM), D ** -0.5, 0.1875, ((0, 8), (1, 4)))
    step_bias = jnp.clip(-2.0 + 3.0 * jax.random.uniform(splits[10], (MHEADS,), jnp.float32) ** level_of(splits[10], (MHEADS,), ((0, 4),), -0.2, 0.2), -2.0, 1.0)
    decay_log = jnp.clip(-12.0 + 9.5 * jax.random.uniform(splits[11], (MHEADS,), jnp.float32) ** level_of(splits[11], (MHEADS,), ((0, 4),), -0.2, 0.2), -12.0, -2.5)
    skip_gain = jnp.clip(0.5 + 1.0 * jax.random.uniform(splits[12], (MHEADS,), jnp.float32) ** level_of(splits[12], (MHEADS,), ((0, 4),), -0.2, 0.2), 0.5, 1.5)
    mixer_out = normal_values(splits[13], (MINNER, D), MINNER ** -0.5, 0.15625, ((0, 4), (1, 8)))
    attn_out = normal_values(splits[14], (QHEADS * HDIM, D), (max(1, QHEADS * HDIM // 8)) ** -0.5, 0.75, ((0, 4), (1, 8)))
    ffn_gate = normal_values(splits[15], (D, FF), D ** -0.5, 0.1875, ((0, 8), (1, 4)))
    ffn_up = normal_values(splits[16], (D, FF), D ** -0.5, 0.1875, ((0, 8), (1, 4)))
    ffn_down = normal_values(splits[17], (FF, D), (max(1, FF // 4)) ** -0.5, 0.25, ((0, 4), (1, 8)))
    return {"tokens": tokens, "lengths": lengths, "cotangent": cotangent, "in_norm_gain": in_norm_gain, "ffn_norm_gain": ffn_norm_gain, "mixer_in": mixer_in, "step_weight": step_weight, "state_proj": state_proj, "keyval_weight": keyval_weight, "query_weight": query_weight, "step_bias": step_bias, "decay_log": decay_log, "skip_gain": skip_gain, "mixer_out": mixer_out, "attn_out": attn_out, "ffn_gate": ffn_gate, "ffn_up": ffn_up, "ffn_down": ffn_down}


EPS = 1e-05
ROPE_BASE = 10000.0
NEG_FILL = -1e+30
exact_dots = lax.Precision.HIGHEST

def widened(operand):
    return lax.optimization_barrier(operand).astype(jnp.float32)

def rounded(operand):
    return widened(operand.astype(jnp.bfloat16))

def angle_tables(places, width):
    half_width = width // 2
    frequencies = ROPE_BASE ** (-(jnp.arange(half_width).astype(jnp.float32) * 2.0 / width))
    angles = places.astype(jnp.float32)[:, None] * frequencies[None, :]
    return (jnp.cos(angles)[:, None, :], jnp.sin(angles)[:, None, :], half_width)

def rotate(vectors, places):
    cosine, sine_part, half_width = angle_tables(places, vectors.shape[-1])
    first_half = vectors[..., :half_width]
    second = vectors[..., half_width:]
    return jnp.concatenate([first_half * cosine - second * sine_part, second * cosine + first_half * sine_part], axis=-1)

def rotate_back(grad_rows, places):
    cosine, sine_part, half_width = angle_tables(places, grad_rows.shape[-1])
    first_half = grad_rows[..., :half_width]
    second = grad_rows[..., half_width:]
    return jnp.concatenate([first_half * cosine + second * sine_part, second * cosine - first_half * sine_part], axis=-1)

def step_decay(step_raw, inputs, step_bias, decay_log, live_mask):
    step_size = jax.nn.softplus(step_raw + step_bias[None, :]) * live_mask[:, None]
    log_decay = -jnp.exp(decay_log)[None, :] * step_size
    driven = inputs * step_size[:, :, None]
    return (log_decay, driven)

def state_space(inputs, gate_pre, b_proj, c_proj, step_raw, step_bias, decay_log, skip_gain, live_mask, state_in):
    row_count, head_count, head_width = inputs.shape
    log_decay, driven = step_decay(step_raw, inputs, step_bias, decay_log, live_mask)
    block_count = row_count // STRETCH
    lower = jnp.arange(STRETCH)[:, None] >= jnp.arange(STRETCH)[None, :]

    def advance(state, pieces):
        decay_part, driven_part, b_part, c_part, input_part = pieces
        cumulative = jnp.cumsum(decay_part, axis=0)
        differences = cumulative[:, None, :] - cumulative[None, :, :]
        decays = jnp.exp(jnp.where(lower[:, :, None], differences, NEG_FILL))
        products = jnp.dot(c_part, b_part.T, precision=exact_dots)
        within = jnp.einsum('ts,tsh,shp->thp', products, decays, driven_part, precision=exact_dots)
        carried = jnp.einsum('tn,hnp->thp', c_part, state, precision=exact_dots) * jnp.exp(cumulative)[:, :, None]
        tail_decay = jnp.exp(cumulative[-1][None, :] - cumulative)
        new_state = jnp.exp(cumulative[-1])[:, None, None] * state + jnp.einsum('sh,sn,shp->hnp', tail_decay, b_part, driven_part, precision=exact_dots)
        return (new_state, within + carried + skip_gain[None, :, None] * input_part)
    state_out, outputs = lax.scan(advance, state_in, (log_decay.reshape(block_count, STRETCH, head_count), driven.reshape(block_count, STRETCH, head_count, head_width), b_proj.reshape(block_count, STRETCH, -1), c_proj.reshape(block_count, STRETCH, -1), inputs.reshape(block_count, STRETCH, head_count, head_width)))
    mixer_y = outputs.reshape(row_count, head_count, head_width)
    return (mixer_y * jax.nn.silu(gate_pre), state_out)

def masked_scores(block_query, keys_f, block_places, places, length, score_scale):
    scores = jnp.einsum('qhd,kd->hqk', block_query, keys_f) * score_scale
    allowed = (places[None, :] <= block_places[:, None]) & (places[None, :] < length)
    return jnp.where(allowed[None], scores, NEG_FILL)

def attend(query_b, key_b, value_b, places, length):
    row_count, head_count, head_width = query_b.shape
    block_rows = min(512, row_count)
    score_scale = head_width ** (-0.5)
    keys_f = widened(key_b)
    values_f = widened(value_b)
    query_f = widened(query_b)

    def one_block(block_index):
        block_query = lax.dynamic_slice_in_dim(query_f, block_index * block_rows, block_rows, 0)
        block_places = lax.dynamic_slice_in_dim(places, block_index * block_rows, block_rows, 0)
        scores = masked_scores(block_query, keys_f, block_places, places, length, score_scale)
        peak_score = lax.optimization_barrier(jnp.max(scores, axis=-1))
        log_total = peak_score + jnp.log(lax.optimization_barrier(jnp.sum(jnp.exp(scores - peak_score[..., None]), axis=-1)))
        prob_rows = rounded(jnp.exp(scores - log_total[..., None]))
        outputs = jnp.einsum('hqk,kd->qhd', prob_rows, values_f)
        return (outputs, log_total)
    outputs, log_totals = lax.map(one_block, jnp.arange(row_count // block_rows))
    return (outputs.reshape(row_count, head_count, head_width), log_totals)

def attend_back(query_b, key_b, value_b, attended_b, dattended_b, log_totals, places, length):
    row_count, head_count, head_width = query_b.shape
    block_rows = min(512, row_count)
    score_scale = head_width ** (-0.5)
    keys_f = widened(key_b)
    values_f = widened(value_b)
    query_f = widened(query_b)
    dout_f = widened(dattended_b)
    row_terms = lax.optimization_barrier(jnp.sum(dout_f * widened(attended_b), axis=-1))

    def one_block(loop_state, block_index):
        dkey, dvalue = loop_state
        start = block_index * block_rows
        block_query = lax.dynamic_slice_in_dim(query_f, start, block_rows, 0)
        block_dout = lax.dynamic_slice_in_dim(dout_f, start, block_rows, 0)
        block_places = lax.dynamic_slice_in_dim(places, start, block_rows, 0)
        block_terms = lax.dynamic_slice_in_dim(row_terms, start, block_rows, 0).T
        scores = masked_scores(block_query, keys_f, block_places, places, length, score_scale)
        prob_rows = jnp.exp(scores - log_totals[block_index][..., None])
        dprob = jnp.einsum('qhd,kd->hqk', block_dout, values_f)
        dscore_f = rounded(prob_rows * (dprob - block_terms[..., None]))
        dquery = jnp.einsum('hqk,kd->qhd', dscore_f, keys_f) * score_scale
        dkey = dkey + jnp.einsum('hqk,qhd->kd', dscore_f, block_query) * score_scale
        dvalue = dvalue + jnp.einsum('hqk,qhd->kd', rounded(prob_rows), block_dout)
        return ((dkey, dvalue), dquery)
    zeros_keys = jnp.zeros((row_count, head_width), jnp.float32)
    (dkey, dvalue), dquery = lax.scan(one_block, (zeros_keys, zeros_keys), jnp.arange(row_count // block_rows))
    return (dquery.reshape(row_count, head_count, head_width), dkey, dvalue)

def reference(tokens, lengths, cotangent, in_norm_gain, ffn_norm_gain, mixer_in, step_weight, state_proj, keyval_weight, query_weight, step_bias, decay_log, skip_gain, mixer_out, attn_out, ffn_gate, ffn_up, ffn_down):
    heads_group = MHEADS // N_TP
    inner_group = heads_group * MDIM
    query_group = QHEADS // N_TP
    query_width = query_group * HDIM
    hidden_group = FF // N_TP
    kv_span = KVHEADS * HDIM
    places = jnp.arange(SEQ_LEN).astype(jnp.int32)
    gain_in = in_norm_gain.astype(jnp.float32)
    gain_ffn = ffn_norm_gain.astype(jnp.float32)

    def one_sequence(totals, seq_item):
        seq_tokens, length, seq_cot = seq_item
        inputs_f = seq_tokens.astype(jnp.float32)
        live_mask = (places < length).astype(jnp.float32)
        inv_one = lax.rsqrt(lax.optimization_barrier(jnp.mean(inputs_f * inputs_f, axis=-1, keepdims=True)) + EPS)
        normed = (inputs_f * inv_one * gain_in).astype(jnp.bfloat16)
        state_cols = jnp.dot(normed, state_proj, preferred_element_type=jnp.float32)
        b_proj = state_cols[:, :STATE]
        c_proj = state_cols[:, STATE:]
        keyval_cols = jnp.dot(normed, keyval_weight, preferred_element_type=jnp.float32)
        step_all = jnp.dot(normed, step_weight, preferred_element_type=jnp.float32)
        mixed = jnp.zeros((SEQ_LEN, D), jnp.float32)
        saved = []
        for group_index in range(N_TP):
            head_slice = slice(group_index * heads_group, (group_index + 1) * heads_group)
            mixer_group = mixer_in[:, :, group_index * inner_group:(group_index + 1) * inner_group].reshape(D, 2 * inner_group)
            projected = jnp.dot(normed, mixer_group, preferred_element_type=jnp.float32).reshape(SEQ_LEN, 2, heads_group, MDIM)

            def mixer_fn(inputs, gate_pre, b_part, c_part, step_raw, bias_part, decay_part, skip_part, state_in):
                return state_space(inputs, gate_pre, b_part, c_part, step_raw, bias_part, decay_part, skip_part, live_mask, state_in)
            state_zero = jnp.zeros((heads_group, STATE, MDIM), jnp.float32)
            (gated, state_end), mixer_back = jax.vjp(mixer_fn, projected[:, 1], projected[:, 0], b_proj, c_proj, step_all[:, head_slice], step_bias[head_slice], decay_log[head_slice], skip_gain[head_slice], state_zero)
            gated_b = gated.astype(jnp.bfloat16).reshape(SEQ_LEN, inner_group)
            kv_head = group_index * query_group // (QHEADS // KVHEADS)
            key_raw = keyval_cols[:, kv_head * HDIM:(kv_head + 1) * HDIM]
            value_raw = keyval_cols[:, kv_span + kv_head * HDIM:kv_span + (kv_head + 1) * HDIM]
            query_cols = slice(group_index * query_width, (group_index + 1) * query_width)
            queries = jnp.dot(normed, query_weight[:, query_cols], preferred_element_type=jnp.float32).reshape(SEQ_LEN, query_group, HDIM)
            query_b = rotate(queries, places).astype(jnp.bfloat16)
            key_b = rotate(key_raw[:, None, :], places)[:, 0].astype(jnp.bfloat16)
            value_b = value_raw.astype(jnp.bfloat16)
            attended, log_totals = attend(query_b, key_b, value_b, places, length)
            attended_b = attended.astype(jnp.bfloat16)
            out_rows = slice(group_index * inner_group, (group_index + 1) * inner_group)
            partial_term = jnp.dot(gated_b, mixer_out[out_rows], preferred_element_type=jnp.float32) + jnp.dot(attended_b.reshape(SEQ_LEN, query_width), attn_out[query_cols], preferred_element_type=jnp.float32)
            mixed = mixed + rounded(partial_term)
            saved.append((head_slice, mixer_group, mixer_back, gated_b, kv_head, query_cols, out_rows, query_b, key_b, value_b, attended_b, log_totals))
        resid = inputs_f + mixed
        inv_two = lax.rsqrt(lax.optimization_barrier(jnp.mean(resid * resid, axis=-1, keepdims=True)) + EPS)
        normed_two = (resid * inv_two * gain_ffn).astype(jnp.bfloat16)
        ffn_total = jnp.zeros((SEQ_LEN, D), jnp.float32)
        ffn_saved = []
        for group_index in range(N_TP):
            hidden_cols = slice(group_index * hidden_group, (group_index + 1) * hidden_group)
            gate_val = jnp.dot(normed_two, ffn_gate[:, hidden_cols], preferred_element_type=jnp.float32)
            up_val = jnp.dot(normed_two, ffn_up[:, hidden_cols], preferred_element_type=jnp.float32)
            act_b = (jax.nn.silu(gate_val) * up_val).astype(jnp.bfloat16)
            ffn_total = ffn_total + rounded(jnp.dot(act_b, ffn_down[hidden_cols], preferred_element_type=jnp.float32))
            ffn_saved.append((hidden_cols, gate_val, up_val, act_b))
        block_out = (resid + ffn_total).astype(jnp.bfloat16)
        dnormed_two = jnp.zeros((SEQ_LEN, D), jnp.float32)
        down_parts, gate_parts, up_parts = ([], [], [])
        for hidden_cols, gate_val, up_val, act_b in ffn_saved:
            act_grad = jnp.dot(seq_cot, ffn_down[hidden_cols].T, preferred_element_type=jnp.float32)
            sigmoid_gate = jax.nn.sigmoid(gate_val)
            dgate_b = (act_grad * up_val * sigmoid_gate * (1.0 + gate_val * (1.0 - sigmoid_gate))).astype(jnp.bfloat16)
            dup_b = (act_grad * gate_val * sigmoid_gate).astype(jnp.bfloat16)
            down_parts.append(jnp.dot(act_b.T, seq_cot, preferred_element_type=jnp.float32))
            gate_parts.append(jnp.dot(normed_two.T, dgate_b, preferred_element_type=jnp.float32))
            up_parts.append(jnp.dot(normed_two.T, dup_b, preferred_element_type=jnp.float32))
            dnormed_two = dnormed_two + rounded(jnp.dot(dgate_b, ffn_gate[:, hidden_cols].T, preferred_element_type=jnp.float32) + jnp.dot(dup_b, ffn_up[:, hidden_cols].T, preferred_element_type=jnp.float32))
        scaled_two = gain_ffn * dnormed_two
        ffn_norm_grad = lax.optimization_barrier(jnp.sum(dnormed_two * resid * inv_two, axis=0))
        dresid = seq_cot.astype(jnp.float32) + inv_two * scaled_two - resid * inv_two ** 3 * lax.optimization_barrier(jnp.mean(scaled_two * resid, axis=-1, keepdims=True))
        dmixed_b = dresid.astype(jnp.bfloat16)
        dnormed = jnp.zeros((SEQ_LEN, D), jnp.float32)
        state_total = jnp.zeros((D, 2 * STATE), jnp.float32)
        keyval_total = jnp.zeros((D, 2 * kv_span), jnp.float32)
        mixer_parts, step_parts, query_parts, out_parts, attn_parts = ([], [], [], [], [])
        bias_parts, decay_parts, skip_parts = ([], [], [])
        for head_slice, mixer_group, mixer_back, gated_b, kv_head, query_cols, out_rows, query_b, key_b, value_b, attended_b, log_totals in saved:
            out_parts.append(jnp.dot(gated_b.T, dmixed_b, preferred_element_type=jnp.float32))
            attn_parts.append(jnp.dot(attended_b.reshape(SEQ_LEN, query_width).T, dmixed_b, preferred_element_type=jnp.float32))
            dgated = jnp.dot(dmixed_b, mixer_out[out_rows].T, preferred_element_type=jnp.float32).reshape(SEQ_LEN, heads_group, MDIM)
            dattended_b = jnp.dot(dmixed_b, attn_out[query_cols].T, preferred_element_type=jnp.float32).reshape(SEQ_LEN, query_group, HDIM).astype(jnp.bfloat16)
            grad_list = mixer_back((dgated, jnp.zeros((heads_group, STATE, MDIM), jnp.float32)))
            dinputs, dgate_pre, db_proj, dc_proj, dstep_raw, dbias, ddecay, dskip, state_unused = grad_list
            dquery, dkey, dvalue = attend_back(query_b, key_b, value_b, attended_b, dattended_b, log_totals, places, length)
            dquery_b = rotate_back(dquery, places).reshape(SEQ_LEN, query_width).astype(jnp.bfloat16)
            dkey_rot = rotate_back(dkey[:, None, :], places)[:, 0]
            dkeyval = jnp.zeros((SEQ_LEN, 2 * kv_span), jnp.float32)
            dkeyval = dkeyval.at[:, kv_head * HDIM:(kv_head + 1) * HDIM].set(dkey_rot)
            dkeyval = dkeyval.at[:, kv_span + kv_head * HDIM:kv_span + (kv_head + 1) * HDIM].set(dvalue)
            dkeyval_b = dkeyval.astype(jnp.bfloat16)
            dstate_b = jnp.concatenate([db_proj, dc_proj], axis=1).astype(jnp.bfloat16)
            dmix_in_b = jnp.stack([dgate_pre, dinputs], axis=1).reshape(SEQ_LEN, 2 * inner_group).astype(jnp.bfloat16)
            dstep_b = dstep_raw.astype(jnp.bfloat16)
            mixer_parts.append(jnp.dot(normed.T, dmix_in_b, preferred_element_type=jnp.float32).reshape(D, 2, inner_group))
            step_parts.append(jnp.dot(normed.T, dstep_b, preferred_element_type=jnp.float32))
            query_parts.append(jnp.dot(normed.T, dquery_b, preferred_element_type=jnp.float32))
            state_total = state_total + jnp.dot(normed.T, dstate_b, preferred_element_type=jnp.float32)
            keyval_total = keyval_total + jnp.dot(normed.T, dkeyval_b, preferred_element_type=jnp.float32)
            group_term = jnp.dot(dmix_in_b, mixer_group.T, preferred_element_type=jnp.float32)
            group_term = group_term + jnp.dot(dstep_b, step_weight[:, head_slice].T, preferred_element_type=jnp.float32)
            group_term = group_term + jnp.dot(dstate_b, state_proj.T, preferred_element_type=jnp.float32)
            group_term = group_term + jnp.dot(dkeyval_b, keyval_weight.T, preferred_element_type=jnp.float32)
            group_term = group_term + jnp.dot(dquery_b, query_weight[:, query_cols].T, preferred_element_type=jnp.float32)
            dnormed = dnormed + rounded(group_term)
            bias_parts.append(dbias)
            decay_parts.append(ddecay)
            skip_parts.append(dskip)
        scaled_one = gain_in * dnormed
        in_norm_grad = lax.optimization_barrier(jnp.sum(dnormed * inputs_f * inv_one, axis=0))
        input_grad = dresid + inv_one * scaled_one - inputs_f * inv_one ** 3 * lax.optimization_barrier(jnp.mean(scaled_one * inputs_f, axis=-1, keepdims=True))
        pieces = (in_norm_grad, ffn_norm_grad, jnp.concatenate(mixer_parts, axis=2), jnp.concatenate(step_parts, axis=1), state_total, keyval_total, jnp.concatenate(query_parts, axis=1), jnp.concatenate(bias_parts), jnp.concatenate(decay_parts), jnp.concatenate(skip_parts), jnp.concatenate(out_parts, axis=0), jnp.concatenate(attn_parts, axis=0), jnp.concatenate(gate_parts, axis=1), jnp.concatenate(up_parts, axis=1), jnp.concatenate(down_parts, axis=0))
        new_totals = tuple((left + right for left, right in zip(totals, pieces)))
        return (new_totals, (block_out, input_grad))
    zero_totals = (jnp.zeros((D,), jnp.float32), jnp.zeros((D,), jnp.float32), jnp.zeros((D, 2, MINNER), jnp.float32), jnp.zeros((D, MHEADS), jnp.float32), jnp.zeros((D, 2 * STATE), jnp.float32), jnp.zeros((D, 2 * kv_span), jnp.float32), jnp.zeros((D, QHEADS * HDIM), jnp.float32), jnp.zeros((MHEADS,), jnp.float32), jnp.zeros((MHEADS,), jnp.float32), jnp.zeros((MHEADS,), jnp.float32), jnp.zeros((MINNER, D), jnp.float32), jnp.zeros((QHEADS * HDIM, D), jnp.float32), jnp.zeros((D, FF), jnp.float32), jnp.zeros((D, FF), jnp.float32), jnp.zeros((FF, D), jnp.float32))
    totals, (block_out, input_grad) = lax.scan(one_sequence, zero_totals, (tokens, lengths, cotangent))
    return (block_out, input_grad, totals[0], totals[1], totals[2], totals[3], totals[4], totals[5], totals[6], totals[7], totals[8], totals[9], totals[10], totals[11], totals[12], totals[13], totals[14])
```

```python
import jax
import jax.numpy as jnp
from jax import lax
from jax.sharding import PartitionSpec as P

MDIM = 64
STATE = 128
QHEADS = 8
KVHEADS = 2
HDIM = 64
STRETCH = 256


EPS = 1e-05
ROPE_BASE = 10000.0
NEG_FILL = -1e30
exact_dots = lax.Precision.HIGHEST


def carried_in(shard, axis, join, neutral, backward):
    count = lax.axis_size(axis)
    place = lax.axis_index(axis)
    ahead = count - 1 - place if backward else place
    gathered = jax.tree.map(
        lambda a, kind: lax.all_gather(a.astype(kind), axis), shard, (jnp.bfloat16, jnp.bfloat16)
    )
    state = jax.tree.map(lambda a, e: jnp.zeros_like(a) + jnp.asarray(e, a.dtype), shard, neutral)

    def one(turn, state):
        source = count - 1 - turn if backward else turn
        return join(
            state,
            jax.tree.map(
                lambda a, own: lax.dynamic_index_in_dim(a, source, 0, False).astype(own.dtype),
                gathered,
                shard,
            ),
        )

    return lax.fori_loop(0, ahead, one, state)


def angle_tables(places, width):
    half_width = width // 2
    frequencies = ROPE_BASE ** (-(jnp.arange(half_width).astype(jnp.float32) * 2.0 / width))
    angles = places.astype(jnp.float32)[:, None] * frequencies[None, :]
    return (jnp.cos(angles)[:, None, :], jnp.sin(angles)[:, None, :], half_width)


def rotate(vectors, places):
    cosine, sine_part, half_width = angle_tables(places, vectors.shape[-1])
    first_half = vectors[..., :half_width]
    second = vectors[..., half_width:]
    return jnp.concatenate(
        [first_half * cosine - second * sine_part, second * cosine + first_half * sine_part],
        axis=-1,
    )


def rotate_back(grad_rows, places):
    cosine, sine_part, half_width = angle_tables(places, grad_rows.shape[-1])
    first_half = grad_rows[..., :half_width]
    second = grad_rows[..., half_width:]
    return jnp.concatenate(
        [first_half * cosine + second * sine_part, second * cosine - first_half * sine_part],
        axis=-1,
    )


def step_decay(step_raw, inputs, step_bias, decay_log, live_mask):
    step_size = jax.nn.softplus(step_raw + step_bias[None, :]) * live_mask[:, None]
    log_decay = -jnp.exp(decay_log)[None, :] * step_size
    driven = inputs * step_size[:, :, None]
    return (log_decay, driven)


def state_space(
    inputs, gate_pre, b_proj, c_proj, step_raw, step_bias, decay_log, skip_gain, live_mask, state_in
):
    row_count, head_count, head_width = inputs.shape
    log_decay, driven = step_decay(step_raw, inputs, step_bias, decay_log, live_mask)
    block_count = row_count // STRETCH
    lower = jnp.arange(STRETCH)[:, None] >= jnp.arange(STRETCH)[None, :]

    def advance(state, pieces):
        decay_part, driven_part, b_part, c_part, input_part = pieces
        cumulative = jnp.cumsum(decay_part, axis=0)
        differences = cumulative[:, None, :] - cumulative[None, :, :]
        decays = jnp.exp(jnp.where(lower[:, :, None], differences, NEG_FILL))
        products = jnp.dot(c_part, b_part.T, precision=exact_dots)
        within = jnp.einsum("ts,tsh,shp->thp", products, decays, driven_part, precision=exact_dots)
        carried = (
            jnp.einsum("tn,hnp->thp", c_part, state, precision=exact_dots)
            * jnp.exp(cumulative)[:, :, None]
        )
        tail_decay = jnp.exp(cumulative[-1][None, :] - cumulative)
        new_state = jnp.exp(cumulative[-1])[:, None, None] * state + jnp.einsum(
            "sh,sn,shp->hnp", tail_decay, b_part, driven_part, precision=exact_dots
        )
        return (new_state, within + carried + skip_gain[None, :, None] * input_part)

    state_out, outputs = lax.scan(
        advance,
        state_in,
        (
            log_decay.reshape(block_count, STRETCH, head_count),
            driven.reshape(block_count, STRETCH, head_count, head_width),
            b_proj.reshape(block_count, STRETCH, -1),
            c_proj.reshape(block_count, STRETCH, -1),
            inputs.reshape(block_count, STRETCH, head_count, head_width),
        ),
    )
    mixer_y = outputs.reshape(row_count, head_count, head_width)
    return (mixer_y * jax.nn.silu(gate_pre), state_out)


def chain_states(earlier, later):
    return (earlier[0] * later[0], later[0][:, None, None] * earlier[1] + later[1])


def per_device(
    tokens,
    lengths,
    cotangent,
    in_norm_gain,
    ffn_norm_gain,
    mixer_in,
    step_weight,
    state_proj,
    keyval_weight,
    query_weight,
    step_bias,
    decay_log,
    skip_gain,
    mixer_out,
    attn_out,
    ffn_gate,
    ffn_up,
    ffn_down,
):
    heads_here = step_weight.shape[1]
    inner_here = heads_here * MDIM
    query_cols = query_weight.shape[1]
    hidden_here = ffn_gate.shape[1]
    state_span = state_proj.shape[1]
    keyval_span = keyval_weight.shape[1]
    shard_rows = tokens.shape[2] // (lax.axis_size("fsdp") * lax.axis_size("ctx"))
    weights_in = jnp.concatenate(
        [
            mixer_in.reshape(shard_rows, -1),
            state_proj,
            keyval_weight,
            query_weight,
            step_weight,
            in_norm_gain[:, None],
            ffn_norm_gain[:, None],
        ],
        axis=1,
    )
    weights_out = jnp.concatenate([mixer_out.T, attn_out.T, ffn_down.T, ffn_gate, ffn_up], axis=1)
    full_in = lax.all_gather(weights_in, ("fsdp", "ctx"), axis=0, tiled=True)
    full_out = lax.all_gather(weights_out, ("fsdp", "ctx"), axis=0, tiled=True)
    mix_end = 2 * inner_here
    state_end = mix_end + state_span
    keyval_end = state_end + keyval_span
    query_end = keyval_end + query_cols
    step_end = query_end + heads_here
    gain_in = full_in[:, step_end]
    gain_ffn = full_in[:, step_end + 1]
    attn_end = inner_here + query_cols
    down_end = attn_end + hidden_here
    gate_end = down_end + hidden_here
    full_mixers_t = full_out[:, :attn_end]
    full_down_t = full_out[:, attn_end:down_end]
    full_gate_up = full_out[:, down_end:]
    width_model = full_out.shape[0]
    row_count = tokens.shape[1]
    query_here = query_weight.shape[1] // HDIM
    kv_span = KVHEADS * HDIM
    ctx_index = lax.axis_index("ctx")
    tp_index = lax.axis_index("tp")
    places = ctx_index * row_count + jnp.arange(row_count, dtype=jnp.int32)
    length = lengths[0]
    live_mask = (places < length).astype(jnp.float32)
    inputs_f = tokens[0].astype(jnp.float32)
    inv_one = lax.rsqrt(jnp.mean(inputs_f * inputs_f, axis=-1, keepdims=True) + EPS)
    normed = (inputs_f * inv_one * gain_in.astype(jnp.float32)).astype(jnp.bfloat16)
    all_cols = jnp.dot(normed, full_in[:, :step_end], preferred_element_type=jnp.float32)
    projected = all_cols[:, :mix_end].reshape(row_count, 2, heads_here, MDIM)
    gate_pre = projected[:, 0]
    inputs = projected[:, 1]
    step_raw = all_cols[:, query_end:]
    b_proj = all_cols[:, mix_end : mix_end + STATE]
    c_proj = all_cols[:, mix_end + STATE : state_end]
    keyval_cols = all_cols[:, state_end:keyval_end]
    kv_head = tp_index * query_here // (QHEADS // KVHEADS)
    key_raw = lax.dynamic_slice_in_dim(keyval_cols, kv_head * HDIM, HDIM, 1)
    value_raw = lax.dynamic_slice_in_dim(keyval_cols, kv_span + kv_head * HDIM, HDIM, 1)
    queries = all_cols[:, keyval_end:query_end].reshape(row_count, query_here, HDIM)
    query_b = rotate(queries, places).astype(jnp.bfloat16)
    key_b = rotate(key_raw[:, None, :], places)[:, 0].astype(jnp.bfloat16)
    own_keyval = jnp.concatenate([key_b, value_raw.astype(jnp.bfloat16)], axis=1)
    all_keyval = lax.all_gather(own_keyval, "ctx", axis=0, tiled=True)
    all_keys = all_keyval[:, :HDIM]
    values = all_keyval[:, HDIM:]
    log_decay, driven = step_decay(step_raw, inputs, step_bias, decay_log, live_mask)
    cumulative = jnp.cumsum(log_decay, axis=0)
    own_decay = jnp.exp(cumulative[-1])
    own_state = jnp.einsum(
        "sh,sn,shp->hnp",
        jnp.exp(cumulative[-1][None, :] - cumulative),
        b_proj,
        driven,
        precision=exact_dots,
    )
    identity = (jnp.ones_like(own_decay), jnp.zeros_like(own_state))
    decay_before, state_in = carried_in(
        (own_decay, own_state), "ctx", chain_states, identity, False
    )

    def mixer_fn(
        input_part,
        gate_part,
        b_part,
        c_part,
        step_part,
        bias_part,
        decay_part,
        skip_part,
        state_part,
    ):
        return state_space(
            input_part,
            gate_part,
            b_part,
            c_part,
            step_part,
            bias_part,
            decay_part,
            skip_part,
            live_mask,
            state_part,
        )

    (gated, state_last), mixer_back = jax.vjp(
        mixer_fn,
        inputs,
        gate_pre,
        b_proj,
        c_proj,
        step_raw,
        step_bias,
        decay_log,
        skip_gain,
        state_in,
    )
    gated_b = gated.astype(jnp.bfloat16).reshape(row_count, inner_here)
    block_rows = min(512, row_count)
    score_scale = HDIM ** (-0.5)
    block_count = (ctx_index + 1) * (row_count // block_rows)

    def key_block(block_index):
        start = block_index * block_rows
        key_part = lax.dynamic_slice_in_dim(all_keys, start, block_rows, 0)
        value_part = lax.dynamic_slice_in_dim(values, start, block_rows, 0)
        scores = (
            jnp.einsum("qhd,kd->hqk", query_b, key_part, preferred_element_type=jnp.float32)
            * score_scale
        )
        key_places = start + jnp.arange(block_rows, dtype=jnp.int32)
        allowed = (key_places[None, :] <= places[:, None]) & (key_places[None, :] < length)
        return (jnp.where(allowed[None], scores, NEG_FILL), key_part, value_part)

    def running_total(block_index, loop_state):
        peak_score, mass_total = loop_state
        scores, key_part, value_part = key_block(block_index)
        new_peak = jnp.maximum(peak_score, jnp.max(scores, axis=-1))
        mass_total = mass_total * jnp.exp(peak_score - new_peak) + jnp.sum(
            jnp.exp(scores - new_peak[..., None]), axis=-1
        )
        return (new_peak, mass_total)

    peak_score, mass_total = lax.fori_loop(
        0,
        block_count,
        running_total,
        (
            jnp.full((query_here, row_count), NEG_FILL, jnp.float32),
            jnp.zeros((query_here, row_count), jnp.float32),
        ),
    )
    log_total = peak_score + jnp.log(mass_total)

    def weighted_sum(block_index, summed):
        scores, key_part, value_part = key_block(block_index)
        prob_b = jnp.exp(scores - log_total[..., None]).astype(jnp.bfloat16)
        return summed + jnp.einsum(
            "hqk,kd->qhd", prob_b, value_part, preferred_element_type=jnp.float32
        )

    attended_b = lax.fori_loop(
        0, block_count, weighted_sum, jnp.zeros((row_count, query_here, HDIM), jnp.float32)
    ).astype(jnp.bfloat16)
    attn_flat_b = attended_b.reshape(row_count, query_here * HDIM)
    mixers_b = jnp.concatenate([gated_b, attn_flat_b], axis=1)
    partial_term = jnp.dot(mixers_b, full_mixers_t.T, preferred_element_type=jnp.float32)
    mixed = lax.psum(partial_term.astype(jnp.bfloat16), "tp").astype(jnp.float32)
    resid = inputs_f + mixed
    inv_two = lax.rsqrt(jnp.mean(resid * resid, axis=-1, keepdims=True) + EPS)
    normed_two = (resid * inv_two * gain_ffn.astype(jnp.float32)).astype(jnp.bfloat16)
    gate_up = jnp.dot(normed_two, full_gate_up, preferred_element_type=jnp.float32)
    gate_val = gate_up[:, :hidden_here]
    up_val = gate_up[:, hidden_here:]
    act_b = (jax.nn.silu(gate_val) * up_val).astype(jnp.bfloat16)
    ffn_term = jnp.dot(act_b, full_down_t.T, preferred_element_type=jnp.float32)
    cot_rows = cotangent[0]
    act_grad = jnp.dot(cot_rows, full_down_t, preferred_element_type=jnp.float32)
    sigmoid_gate = jax.nn.sigmoid(gate_val)
    dgate_b = (act_grad * up_val * sigmoid_gate * (1.0 + gate_val * (1.0 - sigmoid_gate))).astype(
        jnp.bfloat16
    )
    dup_b = (act_grad * gate_val * sigmoid_gate).astype(jnp.bfloat16)
    dgate_up_b = jnp.concatenate([dgate_b, dup_b], axis=1)
    down_grad_t = jnp.dot(cot_rows.T, act_b, preferred_element_type=jnp.float32)
    gate_up_grad = jnp.dot(normed_two.T, dgate_up_b, preferred_element_type=jnp.float32)
    dnormed_two_term = jnp.dot(dgate_up_b, full_gate_up.T, preferred_element_type=jnp.float32)
    ffn_sums = lax.psum(
        jnp.concatenate([dnormed_two_term, ffn_term], axis=1).astype(jnp.bfloat16), "tp"
    ).astype(jnp.float32)
    dnormed_two = ffn_sums[:, :width_model]
    block_out = (resid + ffn_sums[:, width_model:]).astype(jnp.bfloat16)
    scaled_two = gain_ffn.astype(jnp.float32) * dnormed_two
    ffn_norm_grad = jnp.sum(dnormed_two * resid * inv_two, axis=0)
    dresid = (
        cot_rows.astype(jnp.float32)
        + inv_two * scaled_two
        - resid * inv_two**3 * jnp.mean(scaled_two * resid, axis=-1, keepdims=True)
    )
    dmixed_b = dresid.astype(jnp.bfloat16)
    mixers_grad_t = jnp.dot(dmixed_b.T, mixers_b, preferred_element_type=jnp.float32)
    out_rows = lax.psum_scatter(
        jnp.concatenate(
            [mixers_grad_t, down_grad_t, gate_up_grad, ffn_norm_grad[:, None]], axis=1
        ).astype(jnp.bfloat16),
        ("fsdp", "ctx"),
        scatter_dimension=0,
        tiled=True,
    ).astype(jnp.float32)
    dmixers = jnp.dot(dmixed_b, full_mixers_t, preferred_element_type=jnp.float32)
    dgated = dmixers[:, :inner_here].reshape(row_count, heads_here, MDIM)
    dattended_b = (
        dmixers[:, inner_here:].reshape(row_count, query_here, HDIM).astype(jnp.bfloat16)
    )
    dstate_direct = jnp.einsum(
        "sn,sh,shp->hnp",
        c_proj,
        jnp.exp(cumulative),
        dgated * jax.nn.silu(gate_pre),
        precision=exact_dots,
    )
    decay_after, later_grad = carried_in(
        (own_decay, dstate_direct), "ctx", chain_states, identity, True
    )
    dinputs, dgate_pre, db_proj, dc_proj, dstep_raw, dbias, ddecay, dskip, dstate_unused = (
        mixer_back((dgated, later_grad))
    )
    row_terms = jnp.sum(dattended_b.astype(jnp.float32) * attended_b.astype(jnp.float32), axis=-1).T

    def back_block(block_index, loop_state):
        dquery, dkeyval = loop_state
        scores, key_part, value_part = key_block(block_index)
        prob_rows = jnp.exp(scores - log_total[..., None])
        dprob = jnp.einsum(
            "qhd,kd->hqk", dattended_b, value_part, preferred_element_type=jnp.float32
        )
        dscore_b = (prob_rows * (dprob - row_terms[..., None])).astype(jnp.bfloat16)
        dquery = (
            dquery
            + jnp.einsum("hqk,kd->qhd", dscore_b, key_part, preferred_element_type=jnp.float32)
            * score_scale
        )
        dkey_part = (
            jnp.einsum("hqk,qhd->kd", dscore_b, query_b, preferred_element_type=jnp.float32)
            * score_scale
        )
        dvalue_part = jnp.einsum(
            "hqk,qhd->kd",
            prob_rows.astype(jnp.bfloat16),
            dattended_b,
            preferred_element_type=jnp.float32,
        )
        dkeyval = lax.dynamic_update_slice_in_dim(
            dkeyval, jnp.concatenate([dkey_part, dvalue_part], axis=1), block_index * block_rows, 0
        )
        return (dquery, dkeyval)

    dquery, dkeyval = lax.fori_loop(
        0,
        block_count,
        back_block,
        (
            jnp.zeros((row_count, query_here, HDIM), jnp.float32),
            jnp.zeros((all_keyval.shape[0], 2 * HDIM), jnp.float32),
        ),
    )
    all_dkeyval = lax.all_gather(dkeyval.astype(jnp.bfloat16), "ctx", axis=0)
    own_dkeyval = jnp.sum(
        lax.dynamic_slice_in_dim(all_dkeyval, ctx_index * row_count, row_count, 1).astype(
            jnp.float32
        ),
        axis=0,
    )
    dkey_rot = rotate_back(own_dkeyval[:, None, :HDIM], places)[:, 0]
    dkeyval_full = jnp.zeros((row_count, 2 * kv_span), jnp.float32)
    dkeyval_full = lax.dynamic_update_slice_in_dim(dkeyval_full, dkey_rot, kv_head * HDIM, 1)
    dkeyval_full = lax.dynamic_update_slice_in_dim(
        dkeyval_full, own_dkeyval[:, HDIM:], kv_span + kv_head * HDIM, 1
    )
    dkeyval_b = dkeyval_full.astype(jnp.bfloat16)
    dquery_b = (
        rotate_back(dquery, places).reshape(row_count, query_here * HDIM).astype(jnp.bfloat16)
    )
    dstate_b = jnp.concatenate([db_proj, dc_proj], axis=1).astype(jnp.bfloat16)
    dmix_in_b = (
        jnp.stack([dgate_pre, dinputs], axis=1)
        .reshape(row_count, 2 * inner_here)
        .astype(jnp.bfloat16)
    )
    dstep_b = dstep_raw.astype(jnp.bfloat16)
    shared_b = jnp.concatenate([dstate_b, dkeyval_b], axis=1)
    dcols_b = jnp.concatenate([dmix_in_b, shared_b, dquery_b, dstep_b], axis=1)
    group_term = jnp.dot(dcols_b, full_in[:, :step_end].T, preferred_element_type=jnp.float32)
    group_sums = lax.psum(
        jnp.concatenate([group_term.astype(jnp.bfloat16), shared_b], axis=1), "tp"
    )
    dnormed = group_sums[:, :width_model].astype(jnp.float32)
    shared_sum = group_sums[:, width_model:]
    own_grad = jnp.dot(
        normed.T,
        jnp.concatenate([dmix_in_b, dquery_b, dstep_b], axis=1),
        preferred_element_type=jnp.float32,
    )
    shared_grad = jnp.dot(normed.T, shared_sum, preferred_element_type=jnp.float32)
    scaled_one = gain_in.astype(jnp.float32) * dnormed
    in_norm_grad = jnp.sum(dnormed * inputs_f * inv_one, axis=0)
    input_grad = (
        dresid
        + inv_one * scaled_one
        - inputs_f * inv_one**3 * jnp.mean(scaled_one * inputs_f, axis=-1, keepdims=True)
    )
    head_columns = jnp.tile(
        jnp.pad(jnp.stack([dbias, ddecay, dskip], axis=1), ((0, shard_rows - heads_here), (0, 0))),
        (width_model // shard_rows, 1),
    )
    in_rows = lax.psum_scatter(
        jnp.concatenate(
            [own_grad, shared_grad, in_norm_grad[:, None], head_columns], axis=1
        ).astype(jnp.bfloat16),
        ("fsdp", "ctx"),
        scatter_dimension=0,
        tiled=True,
    ).astype(jnp.float32)
    query_stop = mix_end + query_cols
    step_stop = query_stop + heads_here
    state_stop = step_stop + state_span
    keyval_stop = state_stop + keyval_span
    mixer_in_rows = in_rows[:, :mix_end].reshape(shard_rows, 2, inner_here)
    query_rows = in_rows[:, mix_end:query_stop]
    step_rows = in_rows[:, query_stop:step_stop]
    state_rows = in_rows[:, step_stop:state_stop]
    keyval_rows = in_rows[:, state_stop:keyval_stop]
    in_norm_rows = in_rows[:, keyval_stop]
    bias_grad = in_rows[:heads_here, keyval_stop + 1]
    decay_grad = in_rows[:heads_here, keyval_stop + 2]
    skip_grad = in_rows[:heads_here, keyval_stop + 3]
    mixer_out_rows = out_rows[:, :inner_here].T
    attn_out_rows = out_rows[:, inner_here:attn_end].T
    down_rows = out_rows[:, attn_end:down_end].T
    gate_rows = out_rows[:, down_end:gate_end]
    up_rows = out_rows[:, gate_end : gate_end + hidden_here]
    ffn_norm_rows = out_rows[:, gate_end + hidden_here]
    return (
        block_out[None],
        input_grad[None],
        in_norm_rows,
        ffn_norm_rows,
        mixer_in_rows,
        step_rows,
        state_rows,
        keyval_rows,
        query_rows,
        bias_grad,
        decay_grad,
        skip_grad,
        mixer_out_rows,
        attn_out_rows,
        gate_rows,
        up_rows,
        down_rows,
    )


def solution(mesh):
    placed = (
        P("fsdp", "ctx", None),
        P("fsdp"),
        P("fsdp", "ctx", None),
        P(("fsdp", "ctx")),
        P(("fsdp", "ctx")),
        P(("fsdp", "ctx"), None, "tp"),
        P(("fsdp", "ctx"), "tp"),
        P(("fsdp", "ctx"), None),
        P(("fsdp", "ctx"), None),
        P(("fsdp", "ctx"), "tp"),
        P("tp"),
        P("tp"),
        P("tp"),
        P("tp", ("fsdp", "ctx")),
        P("tp", ("fsdp", "ctx")),
        P(("fsdp", "ctx"), "tp"),
        P(("fsdp", "ctx"), "tp"),
        P("tp", ("fsdp", "ctx")),
    )
    return jax.shard_map(
        per_device,
        mesh=mesh,
        in_specs=placed,
        out_specs=(
            P("fsdp", "ctx", None),
            P("fsdp", "ctx", None),
            P(("fsdp", "ctx")),
            P(("fsdp", "ctx")),
            P(("fsdp", "ctx"), None, "tp"),
            P(("fsdp", "ctx"), "tp"),
            P(("fsdp", "ctx"), None),
            P(("fsdp", "ctx"), None),
            P(("fsdp", "ctx"), "tp"),
            P("tp"),
            P("tp"),
            P("tp"),
            P("tp", ("fsdp", "ctx")),
            P("tp", ("fsdp", "ctx")),
            P(("fsdp", "ctx"), "tp"),
            P(("fsdp", "ctx"), "tp"),
            P("tp", ("fsdp", "ctx")),
        ),
        check_vma=False,
    )
```

```python
import jax
import jax.numpy as jnp
from jax import lax
from jax.experimental import pallas as pl
from jax.experimental.pallas import tpu as pltpu
from jax.sharding import PartitionSpec as P

MDIM = 64
STATE = 128
QHEADS = 8
KVHEADS = 2
HDIM = 64
STRETCH = 256


EPS = 1e-05
ROPE_BASE = 10000.0
NEG_FILL = -1e30
exact_dots = lax.Precision.HIGHEST


def across(left, right):
    return lax.dot_general(
        left, right, (((1,), (1,)), ((), ())), preferred_element_type=jnp.float32
    )


def over_rows(left, right):
    return lax.dot_general(
        left, right, (((0,), (0,)), ((), ())), preferred_element_type=jnp.float32
    )


def mixer_forward(gate, inputs, b_part, c_part, step, cum_col, cum_row, skip, state, gated, mixer_y):
    rows = inputs.shape[0]
    b_b = b_part[...].astype(jnp.bfloat16)
    c_b = c_part[...].astype(jnp.bfloat16)
    products = across(c_b, b_b)
    carried = across(c_b, state[...].astype(jnp.bfloat16))
    lower = lax.broadcasted_iota(jnp.int32, (rows, rows), 0) >= lax.broadcasted_iota(
        jnp.int32, (rows, rows), 1
    )
    for head in range(step.shape[1]):
        cols = slice(head * MDIM, (head + 1) * MDIM)
        column = cum_col[:, head : head + 1]
        decays = jnp.exp(jnp.where(lower, column - cum_row[head : head + 1, :], NEG_FILL))
        weights_b = (products * decays).astype(jnp.bfloat16)
        part = inputs[:, cols]
        driven_b = (part * step[:, head : head + 1]).astype(jnp.bfloat16)
        y_part = (
            jnp.dot(weights_b, driven_b, preferred_element_type=jnp.float32)
            + carried[:, cols] * jnp.exp(column)
            + skip[:, cols] * part
        )
        gate_part = gate[:, cols]
        mixer_y[:, cols] = y_part
        gated[:, cols] = (y_part * gate_part * jax.nn.sigmoid(gate_part)).astype(jnp.bfloat16)


def mixer_backward(
    dgated, gate, inputs, mixer_y, b_part, c_part, step, cum_col, cum_row, skip, state, later,
    dmix, dshared, decay_col, decay_row, dstep, dskip,
):
    rows = inputs.shape[0]
    inner = inputs.shape[1]
    b_b = b_part[...].astype(jnp.bfloat16)
    c_b = c_part[...].astype(jnp.bfloat16)
    state_b = state[...].astype(jnp.bfloat16)
    later_b = later[...].astype(jnp.bfloat16)
    products = across(c_b, b_b)
    carried = across(c_b, state_b)
    later_rows = across(b_b, later_b)
    lower = lax.broadcasted_iota(jnp.int32, (rows, rows), 0) >= lax.broadcasted_iota(
        jnp.int32, (rows, rows), 1
    )
    dproducts = jnp.zeros((rows, rows), jnp.float32)
    db_total = jnp.zeros(b_part.shape, jnp.float32)
    dc_total = jnp.zeros(c_part.shape, jnp.float32)
    last_row = lax.broadcasted_iota(jnp.int32, (rows, 1), 0) == rows - 1
    for head in range(step.shape[1]):
        cols = slice(head * MDIM, (head + 1) * MDIM)
        column = cum_col[:, head : head + 1]
        decays = jnp.exp(jnp.where(lower, column - cum_row[head : head + 1, :], NEG_FILL))
        weights = products * decays
        part = inputs[:, cols]
        step_part = step[:, head : head + 1]
        driven = part * step_part
        gate_part = gate[:, cols]
        sigmoid = jax.nn.sigmoid(gate_part)
        dgated_part = dgated[:, cols]
        dy = dgated_part * gate_part * sigmoid
        dgate = dgated_part * mixer_y[:, cols] * sigmoid * (1.0 + gate_part * (1.0 - sigmoid))
        dy_b = dy.astype(jnp.bfloat16)
        growth = jnp.exp(column)
        tail = jnp.exp(cum_col[rows - 1 : rows, head : head + 1] - column)
        later_part = tail * later_rows[:, cols]
        ddriven = over_rows(weights.astype(jnp.bfloat16), dy_b) + later_part
        dweights = across(dy_b, driven.astype(jnp.bfloat16))
        dproducts = dproducts + dweights * decays
        pulls = dweights * weights
        tail_pull = jnp.sum(driven * later_part, axis=1, keepdims=True)
        total = (
            jnp.sum(pulls, axis=1, keepdims=True)
            + growth * jnp.sum(dy * carried[:, cols], axis=1, keepdims=True)
            - tail_pull
        )
        total = total + jnp.where(last_row, jnp.sum(tail_pull, axis=0, keepdims=True), 0.0)
        decay_col[:, head : head + 1] = total
        decay_row[head : head + 1, :] = jnp.sum(pulls, axis=0, keepdims=True)
        dc_total = dc_total + jnp.dot(
            (growth * dy).astype(jnp.bfloat16),
            state_b[cols, :],
            preferred_element_type=jnp.float32,
        )
        db_total = db_total + jnp.dot(
            (tail * driven).astype(jnp.bfloat16),
            later_b[cols, :],
            preferred_element_type=jnp.float32,
        )
        dstep[:, head : head + 1] = jnp.sum(ddriven * part, axis=1, keepdims=True)
        dskip[:, cols] = jnp.sum(dy * part, axis=0, keepdims=True)
        dmix[:, cols] = dgate.astype(jnp.bfloat16)
        dmix[:, inner + head * MDIM : inner + (head + 1) * MDIM] = (
            ddriven * step_part + skip[:, cols] * dy
        ).astype(jnp.bfloat16)
    dproducts_b = dproducts.astype(jnp.bfloat16)
    width = b_part.shape[1]
    dshared[:, :width] = (db_total + over_rows(dproducts_b, c_b)).astype(jnp.bfloat16)
    dshared[:, width:] = (
        dc_total + jnp.dot(dproducts_b, b_b, preferred_element_type=jnp.float32)
    ).astype(jnp.bfloat16)


def on_core(body, results, cost):
    return pl.pallas_call(
        body,
        out_shape=results,
        compiler_params=pltpu.CompilerParams(vmem_limit_bytes=48 * 1024 * 1024),
        cost_estimate=pl.CostEstimate(flops=cost, bytes_accessed=8_000_000, transcendentals=0),
    )


def angle_tables(places, width):
    half_width = width // 2
    frequencies = ROPE_BASE ** (-(jnp.arange(half_width).astype(jnp.float32) * 2.0 / width))
    angles = places.astype(jnp.float32)[:, None] * frequencies[None, :]
    return (jnp.cos(angles)[:, None, :], jnp.sin(angles)[:, None, :], half_width)


def rotate(vectors, places):
    cosine, sine_part, half_width = angle_tables(places, vectors.shape[-1])
    first_half = vectors[..., :half_width]
    second = vectors[..., half_width:]
    return jnp.concatenate(
        [first_half * cosine - second * sine_part, second * cosine + first_half * sine_part],
        axis=-1,
    )


def rotate_back(grad_rows, places):
    cosine, sine_part, half_width = angle_tables(places, grad_rows.shape[-1])
    first_half = grad_rows[..., :half_width]
    second = grad_rows[..., half_width:]
    return jnp.concatenate(
        [first_half * cosine + second * sine_part, second * cosine - first_half * sine_part],
        axis=-1,
    )


def per_device(
    tokens,
    lengths,
    cotangent,
    in_norm_gain,
    ffn_norm_gain,
    mixer_in,
    step_weight,
    state_proj,
    keyval_weight,
    query_weight,
    step_bias,
    decay_log,
    skip_gain,
    mixer_out,
    attn_out,
    ffn_gate,
    ffn_up,
    ffn_down,
):
    heads_here = step_weight.shape[1]
    inner_here = heads_here * MDIM
    query_cols = query_weight.shape[1]
    hidden_here = ffn_gate.shape[1]
    state_span = state_proj.shape[1]
    keyval_span = keyval_weight.shape[1]
    shard_rows = tokens.shape[2] // (lax.axis_size("fsdp") * lax.axis_size("ctx"))
    weights_in = jnp.concatenate(
        [
            mixer_in.reshape(shard_rows, -1),
            state_proj,
            keyval_weight,
            query_weight,
            step_weight,
            in_norm_gain[:, None],
            ffn_norm_gain[:, None],
        ],
        axis=1,
    )
    weights_out = jnp.concatenate([mixer_out.T, attn_out.T, ffn_down.T, ffn_gate, ffn_up], axis=1)
    full_in = lax.all_gather(weights_in, ("fsdp", "ctx"), axis=0, tiled=True)
    full_out = lax.all_gather(weights_out, ("fsdp", "ctx"), axis=0, tiled=True)
    mix_end = 2 * inner_here
    state_end = mix_end + state_span
    keyval_end = state_end + keyval_span
    query_end = keyval_end + query_cols
    step_end = query_end + heads_here
    gain_in = full_in[:, step_end]
    gain_ffn = full_in[:, step_end + 1]
    attn_end = inner_here + query_cols
    down_end = attn_end + hidden_here
    gate_end = down_end + hidden_here
    full_mixers_t = full_out[:, :attn_end]
    full_down_t = full_out[:, attn_end:down_end]
    full_gate_up = full_out[:, down_end:]
    width_model = full_out.shape[0]
    row_count = tokens.shape[1]
    query_here = query_weight.shape[1] // HDIM
    kv_span = KVHEADS * HDIM
    ctx_index = lax.axis_index("ctx")
    tp_index = lax.axis_index("tp")
    places = ctx_index * row_count + jnp.arange(row_count, dtype=jnp.int32)
    length = lengths[0]
    live_mask = (places < length).astype(jnp.float32)
    inputs_f = tokens[0].astype(jnp.float32)
    inv_one = lax.rsqrt(jnp.mean(inputs_f * inputs_f, axis=-1, keepdims=True) + EPS)
    normed = (inputs_f * inv_one * gain_in.astype(jnp.float32)).astype(jnp.bfloat16)
    all_cols = jnp.dot(normed, full_in[:, :step_end], preferred_element_type=jnp.float32)
    gate_pre = all_cols[:, :inner_here]
    inputs = all_cols[:, inner_here:mix_end]
    step_raw = all_cols[:, query_end:]
    b_proj = all_cols[:, mix_end : mix_end + STATE]
    c_proj = all_cols[:, mix_end + STATE : state_end]
    keyval_cols = all_cols[:, state_end:keyval_end]
    kv_head = tp_index * query_here // (QHEADS // KVHEADS)
    key_raw = lax.dynamic_slice_in_dim(keyval_cols, kv_head * HDIM, HDIM, 1)
    value_raw = lax.dynamic_slice_in_dim(keyval_cols, kv_span + kv_head * HDIM, HDIM, 1)
    queries = all_cols[:, keyval_end:query_end].reshape(row_count, query_here, HDIM)
    query_b = rotate(queries, places).astype(jnp.bfloat16)
    key_b = rotate(key_raw[:, None, :], places)[:, 0].astype(jnp.bfloat16)
    own_keyval = jnp.concatenate([key_b, value_raw.astype(jnp.bfloat16)], axis=1)
    step_size = jax.nn.softplus(step_raw + step_bias[None, :]) * live_mask[:, None]
    log_decay = -jnp.exp(decay_log)[None, :] * step_size
    row_places = jnp.arange(row_count)
    below = (row_places[:, None] >= row_places[None, :]).astype(jnp.float32)
    cumulative = jnp.cumsum(log_decay, axis=0)
    cum_row = cumulative.T
    head_wide = lambda values: jnp.repeat(values, MDIM, axis=-1)
    tail_step = jnp.exp(cumulative[-1][None, :] - cumulative) * step_size
    own_state = jnp.dot(
        (inputs * head_wide(tail_step)).astype(jnp.bfloat16).T,
        b_proj.astype(jnp.bfloat16),
        preferred_element_type=jnp.float32,
    )
    own_decay = jnp.pad(jnp.exp(cumulative[-1]), (0, STATE - heads_here))
    sent = jnp.concatenate(
        [
            own_keyval,
            own_state.astype(jnp.bfloat16),
            jnp.broadcast_to(own_decay[None, :], (16, STATE)).astype(jnp.bfloat16),
        ],
        axis=0,
    )
    received = lax.all_gather(sent, "ctx", axis=0)
    all_keyval = received[:, :row_count].reshape(-1, 2 * HDIM)
    all_keys = all_keyval[:, :HDIM]
    values = all_keyval[:, HDIM:]
    state_stop_row = row_count + inner_here
    ctx_count = received.shape[0]
    all_states = received[:, row_count:state_stop_row].astype(jnp.float32)
    all_decays = head_wide(
        received[:, state_stop_row, :heads_here].astype(jnp.float32)
    )[:, :, None]
    state_in = jnp.zeros((inner_here, STATE), jnp.float32)
    for source in range(ctx_count - 1):
        state_in = jnp.where(
            source < ctx_index, all_decays[source] * state_in + all_states[source], state_in
        )
    skip_wide = head_wide(skip_gain)[None, :]
    quadratic = row_count * row_count * inner_here
    gated_b, mixer_y = on_core(
        mixer_forward,
        (
            jax.ShapeDtypeStruct((row_count, inner_here), jnp.bfloat16),
            jax.ShapeDtypeStruct((row_count, inner_here), jnp.float32),
        ),
        20 * quadratic,
    )(gate_pre, inputs, b_proj, c_proj, step_size, cumulative, cum_row, skip_wide, state_in)
    block_rows = min(512, row_count)
    score_scale = HDIM ** (-0.5)
    block_count = (ctx_index + 1) * (row_count // block_rows)

    def key_block(block_index):
        start = block_index * block_rows
        key_part = lax.dynamic_slice_in_dim(all_keys, start, block_rows, 0)
        value_part = lax.dynamic_slice_in_dim(values, start, block_rows, 0)
        scores = (
            jnp.einsum("qhd,kd->hqk", query_b, key_part, preferred_element_type=jnp.float32)
            * score_scale
        )
        key_places = start + jnp.arange(block_rows, dtype=jnp.int32)
        allowed = (key_places[None, :] <= places[:, None]) & (key_places[None, :] < length)
        return (jnp.where(allowed[None], scores, NEG_FILL), key_part, value_part)

    def running_total(block_index, loop_state):
        peak_score, mass_total = loop_state
        scores, key_part, value_part = key_block(block_index)
        new_peak = jnp.maximum(peak_score, jnp.max(scores, axis=-1))
        mass_total = mass_total * jnp.exp(peak_score - new_peak) + jnp.sum(
            jnp.exp(scores - new_peak[..., None]), axis=-1
        )
        return (new_peak, mass_total)

    peak_score, mass_total = lax.fori_loop(
        0,
        block_count,
        running_total,
        (
            jnp.full((query_here, row_count), NEG_FILL, jnp.float32),
            jnp.zeros((query_here, row_count), jnp.float32),
        ),
    )
    log_total = peak_score + jnp.log(mass_total)

    def weighted_sum(block_index, summed):
        scores, key_part, value_part = key_block(block_index)
        prob_b = jnp.exp(scores - log_total[..., None]).astype(jnp.bfloat16)
        return summed + jnp.einsum(
            "hqk,kd->qhd", prob_b, value_part, preferred_element_type=jnp.float32
        )

    attended_b = lax.fori_loop(
        0, block_count, weighted_sum, jnp.zeros((row_count, query_here, HDIM), jnp.float32)
    ).astype(jnp.bfloat16)
    attn_flat_b = attended_b.reshape(row_count, query_here * HDIM)
    mixers_b = jnp.concatenate([gated_b, attn_flat_b], axis=1)
    partial_term = jnp.dot(mixers_b, full_mixers_t.T, preferred_element_type=jnp.float32)
    mixed = lax.psum(partial_term.astype(jnp.bfloat16), "tp").astype(jnp.float32)
    resid = inputs_f + mixed
    inv_two = lax.rsqrt(jnp.mean(resid * resid, axis=-1, keepdims=True) + EPS)
    normed_two = (resid * inv_two * gain_ffn.astype(jnp.float32)).astype(jnp.bfloat16)
    gate_up = jnp.dot(normed_two, full_gate_up, preferred_element_type=jnp.float32)
    gate_val = gate_up[:, :hidden_here]
    up_val = gate_up[:, hidden_here:]
    act_b = (jax.nn.silu(gate_val) * up_val).astype(jnp.bfloat16)
    ffn_term = jnp.dot(act_b, full_down_t.T, preferred_element_type=jnp.float32)
    cot_rows = cotangent[0]
    act_grad = jnp.dot(cot_rows, full_down_t, preferred_element_type=jnp.float32)
    sigmoid_gate = jax.nn.sigmoid(gate_val)
    dgate_b = (act_grad * up_val * sigmoid_gate * (1.0 + gate_val * (1.0 - sigmoid_gate))).astype(
        jnp.bfloat16
    )
    dup_b = (act_grad * gate_val * sigmoid_gate).astype(jnp.bfloat16)
    dgate_up_b = jnp.concatenate([dgate_b, dup_b], axis=1)
    down_grad_t = jnp.dot(cot_rows.T, act_b, preferred_element_type=jnp.float32)
    gate_up_grad = jnp.dot(normed_two.T, dgate_up_b, preferred_element_type=jnp.float32)
    dnormed_two_term = jnp.dot(dgate_up_b, full_gate_up.T, preferred_element_type=jnp.float32)
    ffn_sums = lax.psum(
        jnp.concatenate([dnormed_two_term, ffn_term], axis=1).astype(jnp.bfloat16), "tp"
    ).astype(jnp.float32)
    dnormed_two = ffn_sums[:, :width_model]
    block_out = (resid + ffn_sums[:, width_model:]).astype(jnp.bfloat16)
    scaled_two = gain_ffn.astype(jnp.float32) * dnormed_two
    ffn_norm_grad = jnp.sum(dnormed_two * resid * inv_two, axis=0)
    dresid = (
        cot_rows.astype(jnp.float32)
        + inv_two * scaled_two
        - resid * inv_two**3 * jnp.mean(scaled_two * resid, axis=-1, keepdims=True)
    )
    dmixed_b = dresid.astype(jnp.bfloat16)
    mixers_grad_t = jnp.dot(dmixed_b.T, mixers_b, preferred_element_type=jnp.float32)
    out_rows = lax.psum_scatter(
        jnp.concatenate(
            [
                mixers_grad_t.astype(jnp.bfloat16),
                down_grad_t.astype(jnp.bfloat16),
                gate_up_grad.astype(jnp.bfloat16),
            ],
            axis=1,
        ),
        ("fsdp", "ctx"),
        scatter_dimension=0,
        tiled=True,
    )
    dmixers = jnp.dot(dmixed_b, full_mixers_t, preferred_element_type=jnp.float32)
    dgated = dmixers[:, :inner_here]
    dattended_b = (
        dmixers[:, inner_here:].reshape(row_count, query_here, HDIM).astype(jnp.bfloat16)
    )
    row_terms = jnp.sum(dattended_b.astype(jnp.float32) * attended_b.astype(jnp.float32), axis=-1).T

    def back_block(block_index, loop_state):
        dquery, dkeyval = loop_state
        scores, key_part, value_part = key_block(block_index)
        prob_rows = jnp.exp(scores - log_total[..., None])
        dprob = jnp.einsum(
            "qhd,kd->hqk", dattended_b, value_part, preferred_element_type=jnp.float32
        )
        dscore_b = (prob_rows * (dprob - row_terms[..., None])).astype(jnp.bfloat16)
        dquery = (
            dquery
            + jnp.einsum("hqk,kd->qhd", dscore_b, key_part, preferred_element_type=jnp.float32)
            * score_scale
        )
        dkey_part = (
            jnp.einsum("hqk,qhd->kd", dscore_b, query_b, preferred_element_type=jnp.float32)
            * score_scale
        )
        dvalue_part = jnp.einsum(
            "hqk,qhd->kd",
            prob_rows.astype(jnp.bfloat16),
            dattended_b,
            preferred_element_type=jnp.float32,
        )
        dkeyval = lax.dynamic_update_slice_in_dim(
            dkeyval, jnp.concatenate([dkey_part, dvalue_part], axis=1), block_index * block_rows, 0
        )
        return (dquery, dkeyval)

    dquery, dkeyval = lax.fori_loop(
        0,
        block_count,
        back_block,
        (
            jnp.zeros((row_count, query_here, HDIM), jnp.float32),
            jnp.zeros((all_keyval.shape[0], 2 * HDIM), jnp.float32),
        ),
    )
    dstate_direct = jnp.dot(
        (dgated * jax.nn.silu(gate_pre) * head_wide(jnp.exp(cumulative))).astype(jnp.bfloat16).T,
        c_proj.astype(jnp.bfloat16),
        preferred_element_type=jnp.float32,
    )
    keyval_rows_all = dkeyval.shape[0]
    returned = lax.all_gather(
        jnp.concatenate([dkeyval, dstate_direct], axis=0).astype(jnp.bfloat16), "ctx", axis=0
    )
    own_dkeyval = jnp.sum(
        lax.dynamic_slice_in_dim(returned, ctx_index * row_count, row_count, 1).astype(
            jnp.float32
        ),
        axis=0,
    )
    all_dstates = returned[:, keyval_rows_all:].astype(jnp.float32)
    later_grad = jnp.zeros((inner_here, STATE), jnp.float32)
    for source in range(ctx_count - 1, 0, -1):
        later_grad = jnp.where(
            source > ctx_index, all_decays[source] * later_grad + all_dstates[source], later_grad
        )
    dmix_in_b, dstate_b, decay_col, decay_row, dstep_direct, dskip_wide = on_core(
        mixer_backward,
        (
            jax.ShapeDtypeStruct((row_count, 2 * inner_here), jnp.bfloat16),
            jax.ShapeDtypeStruct((row_count, 2 * STATE), jnp.bfloat16),
            jax.ShapeDtypeStruct((row_count, heads_here), jnp.float32),
            jax.ShapeDtypeStruct((heads_here, row_count), jnp.float32),
            jax.ShapeDtypeStruct((row_count, heads_here), jnp.float32),
            jax.ShapeDtypeStruct((1, inner_here), jnp.float32),
        ),
        60 * quadratic,
    )(
        dgated,
        gate_pre,
        inputs,
        mixer_y,
        b_proj,
        c_proj,
        step_size,
        cumulative,
        cum_row,
        skip_wide,
        state_in,
        later_grad,
    )
    through_state = jnp.exp(cumulative[-1]) * jnp.sum(
        (state_in * later_grad).reshape(heads_here, -1), axis=1
    )
    dcumulative = decay_col - decay_row.T
    dlog_decay = jnp.dot(below.T, dcumulative, precision=exact_dots) + through_state[None, :]
    dstep_size = dstep_direct - jnp.exp(decay_log)[None, :] * dlog_decay
    dstep_raw = dstep_size * live_mask[:, None] * jax.nn.sigmoid(step_raw + step_bias[None, :])
    dbias = jnp.sum(dstep_raw, axis=0)
    ddecay = jnp.sum(dlog_decay * log_decay, axis=0)
    dskip = jnp.sum(dskip_wide.reshape(heads_here, MDIM), axis=1)
    dkey_rot = rotate_back(own_dkeyval[:, None, :HDIM], places)[:, 0]
    dkeyval_full = jnp.zeros((row_count, 2 * kv_span), jnp.float32)
    dkeyval_full = lax.dynamic_update_slice_in_dim(dkeyval_full, dkey_rot, kv_head * HDIM, 1)
    dkeyval_full = lax.dynamic_update_slice_in_dim(
        dkeyval_full, own_dkeyval[:, HDIM:], kv_span + kv_head * HDIM, 1
    )
    dkeyval_b = dkeyval_full.astype(jnp.bfloat16)
    dquery_b = (
        rotate_back(dquery, places).reshape(row_count, query_here * HDIM).astype(jnp.bfloat16)
    )
    dstep_b = dstep_raw.astype(jnp.bfloat16)
    shared_b = jnp.concatenate([dstate_b, dkeyval_b], axis=1)
    dcols_b = jnp.concatenate([dmix_in_b, shared_b, dquery_b, dstep_b], axis=1)
    group_term = jnp.dot(dcols_b, full_in[:, :step_end].T, preferred_element_type=jnp.float32)
    group_term, out_rows = lax.optimization_barrier((group_term, out_rows))
    out_rows = out_rows.astype(jnp.float32)
    group_sums = lax.psum(
        jnp.concatenate([group_term.astype(jnp.bfloat16), shared_b], axis=1), "tp"
    )
    dnormed = group_sums[:, :width_model].astype(jnp.float32)
    shared_sum = group_sums[:, width_model:]
    packed_cols = [dmix_in_b, dquery_b, shared_sum, dstep_b]
    used = step_end
    spare = -(used + 5) % 128 + 5
    grads_in = jnp.dot(
        normed.T,
        jnp.concatenate(packed_cols + [jnp.zeros((row_count, spare), jnp.bfloat16)], axis=1),
        preferred_element_type=jnp.float32,
    )
    scaled_one = gain_in.astype(jnp.float32) * dnormed
    in_norm_grad = jnp.sum(dnormed * inputs_f * inv_one, axis=0)
    input_grad = (
        dresid
        + inv_one * scaled_one
        - inputs_f * inv_one**3 * jnp.mean(scaled_one * inputs_f, axis=-1, keepdims=True)
    )
    head_columns = jnp.tile(
        jnp.pad(jnp.stack([dbias, ddecay, dskip], axis=1), ((0, shard_rows - heads_here), (0, 0))),
        (width_model // shard_rows, 1),
    )
    slot = jnp.arange(used + spare)[None, :] - used
    extra = jnp.where(slot == 0, in_norm_grad[:, None], 0.0)
    extra = jnp.where(slot == 1, ffn_norm_grad[:, None], extra)
    for column in range(3):
        extra = jnp.where(slot == 2 + column, head_columns[:, column : column + 1], extra)
    in_rows = lax.psum_scatter(
        (grads_in + extra).astype(jnp.bfloat16),
        ("fsdp", "ctx"),
        scatter_dimension=0,
        tiled=True,
    ).astype(jnp.float32)
    query_stop = mix_end + query_cols
    state_stop = query_stop + state_span
    keyval_stop = state_stop + keyval_span
    mixer_in_rows = in_rows[:, :mix_end].reshape(shard_rows, 2, inner_here)
    query_rows = in_rows[:, mix_end:query_stop]
    step_rows = in_rows[:, keyval_stop:used]
    state_rows = in_rows[:, query_stop:state_stop]
    keyval_rows = in_rows[:, state_stop:keyval_stop]
    in_norm_rows = in_rows[:, used]
    ffn_norm_rows = in_rows[:, used + 1]
    bias_grad = in_rows[:heads_here, used + 2]
    decay_grad = in_rows[:heads_here, used + 3]
    skip_grad = in_rows[:heads_here, used + 4]
    mixer_out_rows = out_rows[:, :inner_here].T
    attn_out_rows = out_rows[:, inner_here:attn_end].T
    down_rows = out_rows[:, attn_end:down_end].T
    gate_rows = out_rows[:, down_end:gate_end]
    up_rows = out_rows[:, gate_end : gate_end + hidden_here]
    return (
        block_out[None],
        input_grad[None],
        in_norm_rows,
        ffn_norm_rows,
        mixer_in_rows,
        step_rows,
        state_rows,
        keyval_rows,
        query_rows,
        bias_grad,
        decay_grad,
        skip_grad,
        mixer_out_rows,
        attn_out_rows,
        gate_rows,
        up_rows,
        down_rows,
    )


def solution(mesh):
    placed = (
        P("fsdp", "ctx", None),
        P("fsdp"),
        P("fsdp", "ctx", None),
        P(("fsdp", "ctx")),
        P(("fsdp", "ctx")),
        P(("fsdp", "ctx"), None, "tp"),
        P(("fsdp", "ctx"), "tp"),
        P(("fsdp", "ctx"), None),
        P(("fsdp", "ctx"), None),
        P(("fsdp", "ctx"), "tp"),
        P("tp"),
        P("tp"),
        P("tp"),
        P("tp", ("fsdp", "ctx")),
        P("tp", ("fsdp", "ctx")),
        P(("fsdp", "ctx"), "tp"),
        P(("fsdp", "ctx"), "tp"),
        P("tp", ("fsdp", "ctx")),
    )
    return jax.shard_map(
        per_device,
        mesh=mesh,
        in_specs=placed,
        out_specs=(
            P("fsdp", "ctx", None),
            P("fsdp", "ctx", None),
            P(("fsdp", "ctx")),
            P(("fsdp", "ctx")),
            P(("fsdp", "ctx"), None, "tp"),
            P(("fsdp", "ctx"), "tp"),
            P(("fsdp", "ctx"), None),
            P(("fsdp", "ctx"), None),
            P(("fsdp", "ctx"), "tp"),
            P("tp"),
            P("tp"),
            P("tp"),
            P("tp", ("fsdp", "ctx")),
            P("tp", ("fsdp", "ctx")),
            P(("fsdp", "ctx"), "tp"),
            P(("fsdp", "ctx"), "tp"),
            P("tp", ("fsdp", "ctx")),
        ),
        check_vma=False,
    )
```
